256 devices in a mesh: prow: 16 (over y, x), pcol: 16 (over z, core).
Axes of the slice: x: 4, y: 4, z: 8, core: 2. Of those that a mesh axis runs over, the one named last changes fastest.
Arguments:
- trailing: float32 [2, 8192, 2, 8192], P(None, 'prow', None, 'pcol'), may hold values from -6 to 6
- panel: float32 [2, 8192, 512], P(None, 'prow', 'pcol'), may hold values from -4 to 4
- diag_inverse: float32 [512, 512], replicated, as said below
Outputs:
- updated: float32 [2, 8192, 2, 8192], P(None, 'prow', None, 'pcol')
- factor: float32 [2, 8192, 512], P(None, 'prow', 'pcol')
The draws below stay inside these ranges and needn't reach their ends.
Inputs may be any that keep to these rules, and one draw needn't show every extreme that they name: `diag_inverse`: the inverse of the lower Cholesky factor of the leading 512 x 512 block; zero above its diagonal.
All inputs are finite; a program needn't handle non-finite values.
Results may differ from the reference program's by a relative error of at most 0.0003.
Values sent between devices are 32-bit elements; how exact they have to be, the bound alone decides.
No kernel may reach another device: no remote copies, remote signals or barrier semaphores. Data moves between devices by JAX's collectives and lax.ppermute only.
A program may use at most 64 MiB of HBM per device.

```python
import math
import jax
import jax.numpy as jnp
from jax import lax

N = 16384
NB = 512
TR = 2
TC = 2
N_PROW = 16
N_PCOL = 16


def draw_diag_inverse(key, part):
    key = jax.random.fold_in(key, 11)
    key_diag = jax.random.fold_in(key, 1)
    key_off = jax.random.fold_in(key, 2)
    diagonal = jax.random.uniform(key_diag, (NB,), jnp.float32, 1.0, 2.0)
    spread = 0.5
    off = jax.random.normal(key_off, (NB, NB), jnp.float32) * (spread / math.sqrt(NB))
    row_ids = jnp.arange(NB)[:, None]
    col_ids = jnp.arange(NB)[None, :]
    below = jnp.where(row_ids > col_ids, off, jnp.zeros_like(off))
    return below + jnp.diag(diagonal)


def level_of(own_key, shape, shards, least, largest):
    def one(dim, shards_of):
        draws = jax.random.uniform(jax.random.fold_in(jax.random.fold_in(own_key, 6), dim), (shards_of,), jnp.float32, least / len(shards), largest / len(shards))
        return jnp.repeat(jnp.exp(draws), shape[dim] // shards_of).reshape((-1,) + (1,) * (len(shape) - dim - 1))

    factor_of = one(*shards[0])
    for cut in shards[1:]:
        factor_of = factor_of * one(*cut)
    return factor_of


def normal_values(stream_key, dims, scale, most, shards=(), held_as=jnp.bfloat16):
    entries = scale * jax.random.normal(stream_key, dims, jnp.float32)
    if shards:
        entries = entries * level_of(stream_key, dims, shards, -0.22, 0.18)
    return jnp.clip(entries, -most, most).astype(held_as)


def setup_inputs(seed: int = 0) -> dict:
    keys = jax.random.split(jax.random.key(seed), 4)
    return {
        "trailing": normal_values(keys[0], (TR, N_PROW * NB, TC, N_PCOL * NB), 1.0, 6.0, ((1, 16), (3, 16)), jnp.float32),
        "panel": normal_values(keys[1], (TR, N_PROW * NB, NB), 0.25, 4.0, ((1, 16), (2, 16)), jnp.float32),
        "diag_inverse": draw_diag_inverse(jax.random.fold_in(keys[3], 71), 0),
    }


def reference(trailing, panel, diag_inverse):
    rows_all = panel.reshape(N, NB)
    factor = jnp.dot(rows_all, diag_inverse.T, precision=lax.Precision.HIGHEST, preferred_element_type=jnp.float32)
    square = trailing.reshape(N, N)
    tile_col = (jnp.arange(N) // NB).astype(jnp.int32)

    def block_update(tile_row):
        first = (tile_row * NB).astype(jnp.int32)
        left_rows = lax.dynamic_slice_in_dim(factor, first, NB, 0)
        current = lax.dynamic_slice_in_dim(square, first, NB, 0)
        changed = current - jnp.dot(left_rows, factor.T, precision=lax.Precision.HIGHEST, preferred_element_type=jnp.float32)
        return jnp.where(tile_row >= tile_col[None, :], changed, jnp.zeros_like(changed))

    result = lax.map(block_update, jnp.arange(N // NB, dtype=jnp.int32)).reshape(trailing.shape)
    return result, factor.reshape(panel.shape)
```

```python
import jax
import jax.numpy as jnp
from jax import lax
from jax.experimental import pallas as pl
from jax.experimental.pallas import tpu as pltpu
from jax.sharding import PartitionSpec as P

CHIPS_Z = 8
GROUPS = 16
NB = 512
NARROW = 32
LANES = 128
PARTS = NB // LANES
STRIDE = 2 * PARTS


def split(x):
    high = x.astype(jnp.bfloat16)
    low = (x - high.astype(jnp.float32)).astype(jnp.bfloat16)
    return high, low


def product(left, right):
    def one(x, y):
        return jnp.dot(x, y, preferred_element_type=jnp.float32)

    return one(left[0], right[0]) + (one(left[0], right[1]) + one(left[1], right[0]))


def kernel(
    same_ref, other_ref, right_ref, inverse_ref, trailing_ref,
    updated_ref, own_ref,
    block, left_high, left_low, right_high, right_low, inv_high, inv_low, solved,
    in_sem, out_sem,
):
    row = lax.axis_index("prow")
    column = lax.axis_index("pcol")
    z, core = column // 2, column % 2
    beneath = row >= column
    fetch = pltpu.make_async_copy(trailing_ref, block, in_sem)
    fetch.start()

    inv_high[...], inv_low[...] = split(inverse_ref[...])
    for slot in range(CHIPS_Z):
        chip = lax.rem(z + CHIPS_Z - slot, CHIPS_Z)
        for source, where in ((same_ref, core), (other_ref, 1 - core)):
            rows = pl.ds(pl.multiple_of((chip * 2 + where) * NARROW, NARROW), NARROW)
            for a in range(2):
                left_high[a, rows, :], left_low[a, rows, :] = split(source[slot, a])
    for slot in range(GROUPS):
        rows = slice(slot * NARROW, (slot + 1) * NARROW)
        for b in range(2):
            right_high[b, rows, :], right_low[b, rows, :] = split(right_ref[slot, b])

    def solve(high, low):
        half = NB // 2
        upper = product(
            (inv_high[:half, :half], inv_low[:half, :half]),
            (high[:half, :], low[:half, :]),
        )
        lower = product((inv_high[half:, :], inv_low[half:, :]), (high[...], low[...]))
        return jnp.concatenate([upper, lower], 0)

    own_rows = pl.ds(pl.multiple_of(column * NARROW, NARROW), NARROW)
    for a in range(2):
        solved[...] = solve(left_high.at[a], left_low.at[a])
        own_ref[a] = solved[own_rows, :]
        left_high[a], left_low[a] = split(solved[...].T)
    for b in range(2):
        right_high[b], right_low[b] = split(solve(right_high.at[b], right_low.at[b]))
    fetch.wait()

    def lines(a, b, j):
        return pl.ds(a * NB * STRIDE + j * 2 + b, NB, stride=STRIDE)

    def update(a, b):
        change = product((left_high[a], left_low[a]), (right_high[b], right_low[b]))
        for j in range(PARTS):
            at = lines(a, b, j)
            block[at, :] = block[at, :] - change[:, j * LANES : (j + 1) * LANES]

    def clear(a, b):
        for j in range(PARTS):
            block[lines(a, b, j), :] = jnp.zeros((NB, LANES), jnp.float32)

    @pl.when(beneath)
    def _():
        update(0, 0)
        update(1, 1)

    @pl.when(jnp.logical_not(beneath))
    def _():
        clear(0, 0)
        clear(1, 1)

    clear(0, 1)
    update(1, 0)
    send = pltpu.make_async_copy(block, updated_ref, out_sem)
    send.start()
    send.wait()


def local(trailing, panel, diag_inverse):
    piece = panel.transpose(0, 2, 1)
    square = [(r * GROUPS + c, c * GROUPS + r) for r in range(GROUPS) for c in range(GROUPS)]
    turned = lax.ppermute(piece, ("prow", "pcol"), square)

    def around(step):
        return [(i, (i // 2 + step) % CHIPS_Z * 2 + i % 2) for i in range(GROUPS)]

    same = [piece] + [lax.ppermute(piece, "pcol", around(s)) for s in range(1, CHIPS_Z)]
    same = jnp.stack(same)
    other = lax.ppermute(same, "pcol", [(i, i ^ 1) for i in range(GROUPS)])
    right = lax.all_to_all(
        jnp.broadcast_to(turned[None], (GROUPS,) + turned.shape), "prow", 0, 0
    )
    view = trailing.reshape(2, NB, 2, PARTS, LANES).transpose(0, 1, 3, 2, 4)
    view = view.reshape(2 * NB * STRIDE, LANES)
    vmem = pl.BlockSpec(memory_space=pltpu.VMEM)
    hbm = pl.BlockSpec(memory_space=pl.ANY)
    half = pltpu.VMEM((2, NB, NB), jnp.bfloat16)
    updated, own = pl.pallas_call(
        kernel,
        out_shape=[
            jax.ShapeDtypeStruct(view.shape, jnp.float32),
            jax.ShapeDtypeStruct(piece.shape, jnp.float32),
        ],
        in_specs=[vmem, vmem, vmem, vmem, hbm],
        out_specs=[hbm, vmem],
        scratch_shapes=[
            pltpu.VMEM(view.shape, jnp.float32),
            half, half, half, half,
            pltpu.VMEM((NB, NB), jnp.bfloat16),
            pltpu.VMEM((NB, NB), jnp.bfloat16),
            pltpu.VMEM((NB, NB), jnp.float32),
            pltpu.SemaphoreType.DMA,
            pltpu.SemaphoreType.DMA,
        ],
        compiler_params=pltpu.CompilerParams(vmem_limit_bytes=48 * 1024 * 1024),
        name="update",
    )(same, other, right, diag_inverse, view)
    updated = updated.reshape(2, NB, PARTS, 2, LANES).transpose(0, 1, 3, 2, 4)
    return updated.reshape(trailing.shape), own.transpose(0, 2, 1)


def solution(mesh):
    return jax.shard_map(
        local,
        mesh=mesh,
        in_specs=(P(None, "prow", None, "pcol"), P(None, "prow", "pcol"), P()),
        out_specs=(P(None, "prow", None, "pcol"), P(None, "prow", "pcol")),
        check_vma=False,
    )
```

```python
import functools

import jax
import jax.numpy as jnp
import numpy as np
from jax import lax
from jax.experimental import pallas as pl
from jax.experimental.pallas import tpu as pltpu
from jax.sharding import PartitionSpec as P

CHIPS_Z = 8
SIDE = 4
GROUPS = 16
NB = 512
HALF = NB // 2
NARROW = 32
LANES = 128
PARTS = NB // LANES
STRIDE = 2 * PARTS
OFFSETS = (0, -1, 1, 2)
PLACE = (
    (7, 14, 6, 2, 11, 9, 5, 8, 12, 1, 0, 4, 13, 15, 3, 10),
    (1, 12, 4, 15, 10, 7, 14, 3, 2, 0, 13, 6, 5, 8, 9, 11),
    (15, 6, 11, 9, 8, 4, 12, 0, 7, 13, 1, 14, 10, 3, 2, 5),
    (9, 13, 1, 0, 5, 10, 11, 3, 6, 4, 2, 15, 12, 7, 14, 8),
    (1, 3, 13, 14, 8, 5, 10, 15, 2, 6, 9, 7, 4, 0, 11, 12),
    (0, 14, 12, 7, 15, 2, 13, 11, 5, 3, 10, 8, 1, 4, 9, 6),
    (5, 4, 15, 2, 6, 0, 1, 12, 8, 14, 11, 13, 3, 9, 7, 10),
    (2, 8, 3, 6, 1, 9, 13, 14, 12, 15, 10, 0, 11, 5, 7, 4),
    (11, 12, 10, 0, 3, 1, 9, 4, 7, 14, 5, 2, 6, 15, 13, 8),
    (13, 8, 5, 9, 4, 11, 7, 15, 0, 10, 3, 2, 14, 12, 6, 1),
    (7, 15, 11, 10, 14, 13, 5, 2, 6, 9, 12, 8, 1, 0, 4, 3),
    (14, 9, 8, 15, 12, 7, 6, 0, 4, 1, 11, 3, 10, 13, 5, 2),
    (4, 5, 9, 12, 15, 0, 3, 1, 7, 13, 14, 10, 11, 8, 6, 2),
    (3, 10, 0, 1, 14, 12, 8, 2, 4, 5, 7, 9, 6, 15, 11, 13),
    (8, 2, 3, 13, 6, 1, 10, 15, 11, 9, 5, 12, 14, 7, 4, 0),
    (0, 5, 4, 7, 2, 13, 11, 14, 3, 10, 8, 6, 1, 9, 15, 12),
)
PIECE_AT = np.argsort(np.array(PLACE), axis=1).astype(np.int32)


def split(x):
    high = x.astype(jnp.bfloat16)
    low = (x - high.astype(jnp.float32)).astype(jnp.bfloat16)
    return high, low


def product(left, right):
    def one(x, y):
        return jnp.dot(x, y, preferred_element_type=jnp.float32)

    return one(left[0], right[0]) + (one(left[0], right[1]) + one(left[1], right[0]))


def chunk(index):
    return pl.ds(pl.multiple_of(index * NARROW, NARROW), NARROW)


def lines(a, b, j, start=0, count=NB):
    return pl.ds((a * NB + start) * STRIDE + j * 2 + b, count, stride=STRIDE)


def load_kernel(view_ref, piece_ref, inverse_ref, tiles_ref, kept_ref, high_ref, low_ref):
    kept_ref[...] = piece_ref[...]
    high_ref[...], low_ref[...] = split(inverse_ref[...])
    for a in range(2):
        for b in range(a + 1):
            for j in range(PARTS):
                tiles_ref[a + b, :, j * LANES : (j + 1) * LANES] = view_ref[lines(a, b, j), :]


def meet_kernel(count, *refs):
    outs = refs[len(refs) - count :]
    for source, to in zip(refs[:count], outs):
        to[...] = source[...]


def stack_kernel(counts, *refs):
    sources = iter(refs)
    outs = refs[sum(counts):]
    for count, out in zip(counts, outs):
        for slot in range(count):
            out[slot] = next(sources)[...]


def left_kernel(
    chips, other_ref, same_ref, other_four_ref, four_ref, inv_high, inv_low,
    high_ref, low_ref, own_ref,
    panel_high, panel_low, solved,
):
    column = lax.axis_index("pcol")
    z, core = column // 2, column % 2
    for slot, step in enumerate(chips):
        chip = lax.rem(z + CHIPS_Z - step, CHIPS_Z)
        far = slot == len(chips) - 1
        pair = (four_ref, other_four_ref) if far else (same_ref, other_ref)
        for source, where in zip(pair, (core, 1 - core)):
            rows = chunk(chip * 2 + where)
            for a in range(2):
                values = source[a] if far else source[slot, a]
                panel_high[a, rows, :], panel_low[a, rows, :] = split(values)
    for a in range(2):
        high, low = panel_high.at[a], panel_low.at[a]
        solved[:HALF, :] = product(
            (inv_high[:HALF, :HALF], inv_low[:HALF, :HALF]), (high[:HALF, :], low[:HALF, :])
        )
        solved[HALF:, :] = product(
            (inv_high[HALF:, :], inv_low[HALF:, :]), (high[...], low[...])
        )
        own_ref[a] = solved[chunk(column), :]
        high[...], low[...] = split(solved[...].T)
        high_ref[a, :, :HALF], low_ref[a, :, :HALF] = split(
            product((high[...], low[...]), (inv_high[:, :HALF], inv_low[:, :HALF]))
        )
        high_ref[a, :, HALF:], low_ref[a, :, HALF:] = split(
            product(
                (high[:, HALF:], low[:, HALF:]), (inv_high[HALF:, HALF:], inv_low[HALF:, HALF:])
            )
        )


def right_kernel(
    table_ref, second_ref, third_ref, fourth_ref, left_high, left_low, first_ref, tiles_ref,
    updated_ref,
    block, panel_high, panel_low, out_sem,
):
    row = lax.axis_index("prow")
    column = lax.axis_index("pcol")
    beneath = row >= column
    y, x, core = row // SIDE, row % SIDE, column % 2

    def place(b):
        for group, source in enumerate((first_ref, second_ref, third_ref, fourth_ref)):
            for slot in range(SIDE):
                to_y = jnp.where(core == 0, OFFSETS[group], OFFSETS[slot])
                to_x = jnp.where(core == 0, OFFSETS[slot], OFFSETS[group])
                at = lax.rem(y + to_y + SIDE, SIDE) * SIDE + lax.rem(x + to_x + SIDE, SIDE)
                rows = chunk(table_ref[column * GROUPS + at])
                panel_high[b, rows, :], panel_low[b, rows, :] = split(source[slot, b])

    def update(a, b, half):
        rows = slice(half * HALF, (half + 1) * HALF)
        change = product(
            (left_high[a, rows, :], left_low[a, rows, :]), (panel_high[b], panel_low[b])
        )
        result = tiles_ref[a + b, rows, :] - change
        for j in range(PARTS):
            block[lines(a, b, j, half * HALF, HALF), :] = result[:, j * LANES : (j + 1) * LANES]

    def clear(a, b, half):
        for j in range(PARTS):
            block[lines(a, b, j, half * HALF, HALF), :] = jnp.zeros((HALF, LANES), jnp.float32)

    def send(a, half):
        part = pl.ds((a * NB + half * HALF) * STRIDE, HALF * STRIDE)
        return pltpu.make_async_copy(
            block.at[part], updated_ref.at[part], out_sem.at[a * 2 + half]
        )

    place(0)
    for half in range(2):
        clear(0, 1, half)

        @pl.when(beneath)
        def _():
            update(0, 0, half)

        @pl.when(jnp.logical_not(beneath))
        def _():
            clear(0, 0, half)

        send(0, half).start()

    @pl.when(beneath)
    def _():
        place(1)

    for half in range(2):
        update(1, 0, half)

        @pl.when(beneath)
        def _():
            update(1, 1, half)

        @pl.when(jnp.logical_not(beneath))
        def _():
            clear(1, 1, half)

        send(1, half).start()
    for a in range(2):
        for half in range(2):
            send(a, half).wait()


VMEM = pl.BlockSpec(memory_space=pltpu.VMEM)
HBM = pl.BlockSpec(memory_space=pl.ANY)
SMEM = pl.BlockSpec(memory_space=pltpu.SMEM)


def params(mib):
    return pltpu.CompilerParams(vmem_limit_bytes=mib * 1024 * 1024)


def along_z(step):
    return [(i, (i // 2 + step) % CHIPS_Z * 2 + i % 2) for i in range(GROUPS)]


def in_plane(move, piece):
    pairs = []
    for r in range(GROUPS):
        for c in range(GROUPS):
            dy, dx = move if c % 2 == 0 else move[::-1]
            to = (r // SIDE + dy) % SIDE * SIDE + (r % SIDE + dx) % SIDE
            pairs.append((r * GROUPS + c, to * GROUPS + c))
    return lax.ppermute(piece, ("prow", "pcol"), pairs)


def cost(flops, elements):
    return pl.CostEstimate(flops=flops, transcendentals=0, bytes_accessed=4 * elements)


def like(*arrays):
    return [jax.ShapeDtypeStruct(a.shape, a.dtype) for a in arrays]


def meet(pieces, others=()):
    return pl.pallas_call(
        functools.partial(meet_kernel, len(pieces)),
        out_shape=like(*pieces),
        in_specs=[VMEM] * len(pieces) + [HBM] * len(others),
        out_specs=[VMEM] * len(pieces),
        compiler_params=params(4),
        cost_estimate=cost(0, 2 * sum(p.size for p in pieces)),
        name="meet",
    )(*pieces, *others)


def stacked(*groups):
    pieces = [p for group in groups for p in group]
    return pl.pallas_call(
        functools.partial(stack_kernel, [len(group) for group in groups]),
        out_shape=[
            jax.ShapeDtypeStruct((len(group),) + group[0].shape, jnp.float32)
            for group in groups
        ],
        in_specs=[VMEM] * len(pieces),
        out_specs=[VMEM] * len(groups),
        compiler_params=params(4),
        cost_estimate=cost(0, 2 * sum(p.size for p in pieces)),
        name="stack",
    )(*pieces)


def local(trailing, panel, diag_inverse):
    piece = panel.transpose(0, 2, 1)
    view = trailing.reshape(2, NB, 2, PARTS, LANES).transpose(0, 1, 3, 2, 4)
    view = view.reshape(2 * NB * STRIDE, LANES)
    whole = jax.ShapeDtypeStruct((NB, NB), jnp.bfloat16)
    pair = jax.ShapeDtypeStruct((2, NB, NB), jnp.bfloat16)

    def by(step, block):
        return lax.ppermute(block, "pcol", along_z(step))

    def swap(block):
        return lax.ppermute(block, "pcol", [(i, i ^ 1) for i in range(GROUPS)])

    tiles, kept, inv_high, inv_low = pl.pallas_call(
        load_kernel,
        out_shape=[jax.ShapeDtypeStruct((3, NB, NB), jnp.float32), *like(piece), whole, whole],
        in_specs=[VMEM] * 3,
        out_specs=[VMEM] * 4,
        compiler_params=params(12),
        cost_estimate=cost(0, 8 * NB * NB),
        name="load",
    )(view, piece, diag_inverse)

    one, seven = by(1, piece), by(-1, piece)
    two, six = by(1, one), by(-1, seven)
    turn = [
        (r * GROUPS + c, PLACE[r][c] * GROUPS + r)
        for r in range(GROUPS)
        for c in range(GROUPS)
    ]
    turned = lax.ppermute(piece, ("prow", "pcol"), turn)
    one, seven, two, six, turned = meet([one, seven, two, six, turned], [tiles])

    three, five = by(1, two), by(-1, six)
    planar = [in_plane(m, turned) for m in ((0, 1), (0, -1), (0, 2))]
    same, first = stacked([kept, one, seven, two, six, three, five], [turned] + planar)

    four = by(1, same[5])
    other, other_four = swap(same), swap(four)
    rest = [in_plane(m, first) for m in ((1, 0), (-1, 0), (2, 0))]
    left_high, left_low, own = pl.pallas_call(
        functools.partial(left_kernel, (0, 1, 7, 2, 6, 3, 5, 4)),
        out_shape=[pair, pair, *like(piece)],
        in_specs=[VMEM] * 6,
        out_specs=[VMEM] * 3,
        scratch_shapes=[
            pltpu.VMEM(pair.shape, pair.dtype),
            pltpu.VMEM(pair.shape, pair.dtype),
            pltpu.VMEM((NB, NB), jnp.float32),
        ],
        compiler_params=params(16),
        cost_estimate=cost(20 * NB**3, 6 * NB * NB),
        name="left",
    )(other, same, other_four, four, inv_high, inv_low)

    updated = pl.pallas_call(
        right_kernel,
        out_shape=jax.ShapeDtypeStruct(view.shape, jnp.float32),
        in_specs=[SMEM] + [VMEM] * 7,
        out_specs=HBM,
        scratch_shapes=[
            pltpu.VMEM(view.shape, jnp.float32),
            pltpu.VMEM(pair.shape, pair.dtype),
            pltpu.VMEM(pair.shape, pair.dtype),
            pltpu.SemaphoreType.DMA((4,)),
        ],
        compiler_params=params(16),
        cost_estimate=cost(18 * NB**3, 12 * NB * NB),
        name="right",
    )(jnp.asarray(PIECE_AT.reshape(-1)), *rest, left_high, left_low, first, tiles)
    updated = updated.reshape(2, NB, PARTS, 2, LANES).transpose(0, 1, 3, 2, 4)
    return updated.reshape(trailing.shape), own.transpose(0, 2, 1)


def solution(mesh):
    return jax.shard_map(
        local,
        mesh=mesh,
        in_specs=(P(None, "prow", None, "pcol"), P(None, "prow", "pcol"), P()),
        out_specs=(P(None, "prow", None, "pcol"), P(None, "prow", "pcol")),
        check_vma=False,
    )
```

```python
import functools

import jax
import jax.numpy as jnp
import numpy as np
from jax import lax
from jax.experimental import pallas as pl
from jax.experimental.pallas import tpu as pltpu
from jax.sharding import PartitionSpec as P

CHIPS_Z = 8
SIDE = 4
GROUPS = 16
NB = 512
HALF = NB // 2
NARROW = 32
LANES = 128
PARTS = NB // LANES
STRIDE = 2 * PARTS
OFFSETS = (0, -1, 1, 2)
PLACE = (
    (7, 14, 6, 2, 11, 9, 5, 8, 12, 1, 0, 4, 13, 15, 3, 10),
    (1, 12, 4, 15, 10, 7, 14, 3, 2, 0, 13, 6, 5, 8, 9, 11),
    (15, 6, 11, 9, 8, 4, 12, 0, 7, 13, 1, 14, 10, 3, 2, 5),
    (9, 13, 1, 0, 5, 10, 11, 3, 6, 4, 2, 15, 12, 7, 14, 8),
    (1, 3, 13, 14, 8, 5, 10, 15, 2, 6, 9, 7, 4, 0, 11, 12),
    (0, 14, 12, 7, 15, 2, 13, 11, 5, 3, 10, 8, 1, 4, 9, 6),
    (5, 4, 15, 2, 6, 0, 1, 12, 8, 14, 11, 13, 3, 9, 7, 10),
    (2, 8, 3, 6, 1, 9, 13, 14, 12, 15, 10, 0, 11, 5, 7, 4),
    (11, 12, 10, 0, 3, 1, 9, 4, 7, 14, 5, 2, 6, 15, 13, 8),
    (13, 8, 5, 9, 4, 11, 7, 15, 0, 10, 3, 2, 14, 12, 6, 1),
    (7, 15, 11, 10, 14, 13, 5, 2, 6, 9, 12, 8, 1, 0, 4, 3),
    (14, 9, 8, 15, 12, 7, 6, 0, 4, 1, 11, 3, 10, 13, 5, 2),
    (4, 5, 9, 12, 15, 0, 3, 1, 7, 13, 14, 10, 11, 8, 6, 2),
    (3, 10, 0, 1, 14, 12, 8, 2, 4, 5, 7, 9, 6, 15, 11, 13),
    (8, 2, 3, 13, 6, 1, 10, 15, 11, 9, 5, 12, 14, 7, 4, 0),
    (0, 5, 4, 7, 2, 13, 11, 14, 3, 10, 8, 6, 1, 9, 15, 12),
)
PIECE_AT = np.argsort(np.array(PLACE), axis=1)
PIECE_WORDS = [
    [
        int(np.array(sum(int(p) << 4 * i for i, p in enumerate(row[at : at + 8])), np.uint32).astype(np.int32))
        for row in PIECE_AT
    ]
    for at in (0, 8)
]


def split(x):
    high = x.astype(jnp.bfloat16)
    low = (x - high.astype(jnp.float32)).astype(jnp.bfloat16)
    return high, low


def product(left, right):
    def one(x, y):
        return jnp.dot(x, y, preferred_element_type=jnp.float32)

    return one(left[0], right[0]) + (one(left[0], right[1]) + one(left[1], right[0]))


def chunk(index):
    return pl.ds(pl.multiple_of(index * NARROW, NARROW), NARROW)


def lines(a, b, j, start=0, count=NB):
    return pl.ds((a * NB + start) * STRIDE + j * 2 + b, count, stride=STRIDE)


def load_kernel(view_ref, piece_ref, inverse_ref, tiles_ref, kept_ref, high_ref, low_ref):
    kept_ref[...] = piece_ref[...]
    high_ref[...], low_ref[...] = split(inverse_ref[...])
    for a in range(2):
        for b in range(a + 1):
            for j in range(PARTS):
                tiles_ref[a + b, :, j * LANES : (j + 1) * LANES] = view_ref[lines(a, b, j), :]


def meet_kernel(count, *refs):
    outs = refs[len(refs) - count :]
    for source, to in zip(refs[:count], outs):
        to[...] = source[...]


def stack_kernel(groups, *refs):
    sources = iter(refs)
    for group, out in zip(groups, refs[len(refs) - len(groups) :]):
        at = 0
        for count in group:
            out[at : at + count] = next(sources)[...]
            at += count


def left_kernel(
    steps, *refs,
):
    count = len(steps)
    blocks, others, (inv_high, inv_low) = refs[:count], refs[count : 2 * count], refs[2 * count : 2 * count + 2]
    high_ref, low_ref, own_ref, panel_high, panel_low, solved = refs[2 * count + 2 :]
    column = lax.axis_index("pcol")
    z, core = column // 2, column % 2
    for which in range(count):
        for slot, step in enumerate(steps[which]):
            chip = lax.rem(z + CHIPS_Z - step, CHIPS_Z)
            for source, where in ((blocks[which], core), (others[which], 1 - core)):
                rows = chunk(chip * 2 + where)
                for a in range(2):
                    panel_high[a, rows, :], panel_low[a, rows, :] = split(source[slot, a])
    for a in range(2):
        high, low = panel_high.at[a], panel_low.at[a]
        solved[:HALF, :] = product(
            (inv_high[:HALF, :HALF], inv_low[:HALF, :HALF]), (high[:HALF, :], low[:HALF, :])
        )
        solved[HALF:, :] = product(
            (inv_high[HALF:, :], inv_low[HALF:, :]), (high[...], low[...])
        )
        own_ref[0, a] = solved[chunk(column), :]
        high[...], low[...] = split(solved[...].T)
        high_ref[a, :, :HALF], low_ref[a, :, :HALF] = split(
            product((high[...], low[...]), (inv_high[:, :HALF], inv_low[:, :HALF]))
        )
        high_ref[a, :, HALF:], low_ref[a, :, HALF:] = split(
            product(
                (high[:, HALF:], low[:, HALF:]), (inv_high[HALF:, HALF:], inv_low[HALF:, HALF:])
            )
        )


def right_kernel(
    first_ref, second_ref, third_ref, fourth_ref, left_high, left_low, tiles_ref,
    updated_ref,
    block, panel_high, panel_low, out_sem,
):
    row = lax.axis_index("prow")
    column = lax.axis_index("pcol")
    beneath = row >= column
    y, x, core = row // SIDE, row % SIDE, column % 2

    def word(entries):
        picked = jnp.int32(0)
        for c, entry in enumerate(entries):
            picked = jnp.where(column == c, jnp.int32(entry), picked)
        return picked

    near, far = word(PIECE_WORDS[0]), word(PIECE_WORDS[1])

    def place(b):
        for group, source in enumerate((first_ref, second_ref, third_ref, fourth_ref)):
            for slot in range(SIDE):
                to_y = jnp.where(core == 0, OFFSETS[group], OFFSETS[slot])
                to_x = jnp.where(core == 0, OFFSETS[slot], OFFSETS[group])
                at = lax.rem(y + to_y + SIDE, SIDE) * SIDE + lax.rem(x + to_x + SIDE, SIDE)
                bits = lax.shift_right_logical(jnp.where(at < 8, near, far), at % 8 * 4)
                rows = chunk(bits & 15)
                panel_high[b, rows, :], panel_low[b, rows, :] = split(source[slot, b])

    def update(a, b, half):
        rows = slice(half * HALF, (half + 1) * HALF)
        change = product(
            (left_high[a, rows, :], left_low[a, rows, :]), (panel_high[b], panel_low[b])
        )
        result = tiles_ref[a + b, rows, :] - change
        for j in range(PARTS):
            block[lines(a, b, j, half * HALF, HALF), :] = result[:, j * LANES : (j + 1) * LANES]

    def clear(a, b, half):
        for j in range(PARTS):
            block[lines(a, b, j, half * HALF, HALF), :] = jnp.zeros((HALF, LANES), jnp.float32)

    def send(a, half):
        part = pl.ds((a * NB + half * HALF) * STRIDE, HALF * STRIDE)
        return pltpu.make_async_copy(
            block.at[part], updated_ref.at[part], out_sem.at[a * 2 + half]
        )

    place(0)
    for half in range(2):
        clear(0, 1, half)

        @pl.when(beneath)
        def _():
            update(0, 0, half)

        @pl.when(jnp.logical_not(beneath))
        def _():
            clear(0, 0, half)

        send(0, half).start()

    @pl.when(beneath)
    def _():
        place(1)

    for half in range(2):
        update(1, 0, half)

        @pl.when(beneath)
        def _():
            update(1, 1, half)

        @pl.when(jnp.logical_not(beneath))
        def _():
            clear(1, 1, half)

        send(1, half).start()
    for a in range(2):
        for half in range(2):
            send(a, half).wait()


VMEM = pl.BlockSpec(memory_space=pltpu.VMEM)
HBM = pl.BlockSpec(memory_space=pl.ANY)


def params(mib):
    return pltpu.CompilerParams(vmem_limit_bytes=mib * 1024 * 1024)


def along_z(step):
    return [(i, (i // 2 + step) % CHIPS_Z * 2 + i % 2) for i in range(GROUPS)]


def in_plane(move, piece):
    pairs = []
    for r in range(GROUPS):
        for c in range(GROUPS):
            dy, dx = move if c % 2 == 0 else move[::-1]
            to = (r // SIDE + dy) % SIDE * SIDE + (r % SIDE + dx) % SIDE
            pairs.append((r * GROUPS + c, to * GROUPS + c))
    return lax.ppermute(piece, ("prow", "pcol"), pairs)


def cost(flops, elements):
    return pl.CostEstimate(flops=flops, transcendentals=0, bytes_accessed=4 * elements)


def like(*arrays):
    return [jax.ShapeDtypeStruct(a.shape, a.dtype) for a in arrays]


def meet(pieces, others=(), hint=0):
    return pl.pallas_call(
        functools.partial(meet_kernel, len(pieces)),
        out_shape=like(*pieces),
        in_specs=[VMEM] * len(pieces) + [HBM] * len(others),
        out_specs=[VMEM] * len(pieces),
        compiler_params=params(4),
        cost_estimate=cost(0, hint or 2 * sum(p.size for p in pieces)),
        name="meet",
    )(*pieces, *others)


def stacked(*groups, others=(), hint=0):
    pieces = [p for group in groups for p in group]
    sizes = [[p.shape[0] for p in group] for group in groups]
    return pl.pallas_call(
        functools.partial(stack_kernel, sizes),
        out_shape=[
            jax.ShapeDtypeStruct((sum(size),) + group[0].shape[1:], jnp.float32)
            for size, group in zip(sizes, groups)
        ],
        in_specs=[VMEM] * len(pieces) + [HBM] * len(others),
        out_specs=[VMEM] * len(groups),
        compiler_params=params(4),
        cost_estimate=cost(0, hint or 2 * sum(p.size for p in pieces)),
        name="stack",
    )(*pieces, *others)


def local(trailing, panel, diag_inverse):
    piece = panel.transpose(0, 2, 1)[None]
    view = trailing.reshape(2, NB, 2, PARTS, LANES).transpose(0, 1, 3, 2, 4)
    view = view.reshape(2 * NB * STRIDE, LANES)
    whole = jax.ShapeDtypeStruct((NB, NB), jnp.bfloat16)
    pair = jax.ShapeDtypeStruct((2, NB, NB), jnp.bfloat16)

    def by(step, block):
        return lax.ppermute(block, "pcol", along_z(step))

    def swap(block):
        return lax.ppermute(block, "pcol", [(i, i ^ 1) for i in range(GROUPS)])

    tiles, kept, inv_high, inv_low = pl.pallas_call(
        load_kernel,
        out_shape=[jax.ShapeDtypeStruct((3, NB, NB), jnp.float32), *like(piece), whole, whole],
        in_specs=[VMEM] * 3,
        out_specs=[VMEM] * 4,
        compiler_params=params(12),
        cost_estimate=cost(0, 8 * NB * NB),
        name="load",
    )(view, piece, diag_inverse)

    turn = [
        (r * GROUPS + c, PLACE[r][c] * GROUPS + r)
        for r in range(GROUPS)
        for c in range(GROUPS)
    ]
    turned = lax.ppermute(piece, ("prow", "pcol"), turn)
    one, seven = by(1, piece), by(-1, piece)
    two, six = by(1, one), by(-1, seven)
    (turned,) = meet([turned], hint=16777216)
    (turned,) = meet([turned], [tiles, one, seven])
    planar = [in_plane(m, turned) for m in ((0, 1), (0, -1), (0, 2))]
    two, six = meet([two, six], [turned])
    three, five = by(1, two), by(-1, six)
    (first,) = stacked([turned] + planar, others=[two, six], hint=16777216)
    (same,) = stacked([kept, one, seven, two, six, three, five], others=[first])
    four = by(1, same[5:6])
    other, other_four = swap(same), swap(four)
    rest = [in_plane(m, first) for m in ((1, 0), (-1, 0), (2, 0))]
    left_high, left_low, own = pl.pallas_call(
        functools.partial(left_kernel, ((0, 1, 7, 2, 6, 3, 5), (4,))),
        out_shape=[pair, pair, *like(piece)],
        in_specs=[VMEM] * 6,
        out_specs=[VMEM] * 3,
        scratch_shapes=[
            pltpu.VMEM(pair.shape, pair.dtype),
            pltpu.VMEM(pair.shape, pair.dtype),
            pltpu.VMEM((NB, NB), jnp.float32),
        ],
        compiler_params=params(16),
        cost_estimate=cost(20 * NB**3, 6 * NB * NB),
        name="left",
    )(same, four, other, other_four, inv_high, inv_low)

    updated = pl.pallas_call(
        right_kernel,
        out_shape=jax.ShapeDtypeStruct(view.shape, jnp.float32),
        in_specs=[VMEM] * 7,
        out_specs=HBM,
        scratch_shapes=[
            pltpu.VMEM(view.shape, jnp.float32),
            pltpu.VMEM(pair.shape, pair.dtype),
            pltpu.VMEM(pair.shape, pair.dtype),
            pltpu.SemaphoreType.DMA((4,)),
        ],
        compiler_params=params(16),
        cost_estimate=cost(18 * NB**3, 12 * NB * NB),
        name="right",
    )(first, *rest, left_high, left_low, tiles)
    updated = updated.reshape(2, NB, PARTS, 2, LANES).transpose(0, 1, 3, 2, 4)
    return updated.reshape(trailing.shape), own[0].transpose(0, 2, 1)


def solution(mesh):
    return jax.shard_map(
        local,
        mesh=mesh,
        in_specs=(P(None, "prow", None, "pcol"), P(None, "prow", "pcol"), P()),
        out_specs=(P(None, "prow", None, "pcol"), P(None, "prow", "pcol")),
        check_vma=False,
    )
```

```python
import functools

import jax
import jax.numpy as jnp
import numpy as np
from jax import lax
from jax.experimental import pallas as pl
from jax.experimental.pallas import tpu as pltpu
from jax.sharding import PartitionSpec as P

CHIPS_Z = 8
SIDE = 4
GROUPS = 16
NB = 512
HALF = NB // 2
NARROW = 32
LANES = 128
PARTS = NB // LANES
STRIDE = 2 * PARTS
OFFSETS = (0, -1, 1, 2)
PLACE = (
    (7, 14, 6, 2, 11, 9, 5, 8, 12, 1, 0, 4, 13, 15, 3, 10),
    (1, 12, 4, 15, 10, 7, 14, 3, 2, 0, 13, 6, 5, 8, 9, 11),
    (15, 6, 11, 9, 8, 4, 12, 0, 7, 13, 1, 14, 10, 3, 2, 5),
    (9, 13, 1, 0, 5, 10, 11, 3, 6, 4, 2, 15, 12, 7, 14, 8),
    (1, 3, 13, 14, 8, 5, 10, 15, 2, 6, 9, 7, 4, 0, 11, 12),
    (0, 14, 12, 7, 15, 2, 13, 11, 5, 3, 10, 8, 1, 4, 9, 6),
    (5, 4, 15, 2, 6, 0, 1, 12, 8, 14, 11, 13, 3, 9, 7, 10),
    (2, 8, 3, 6, 1, 9, 13, 14, 12, 15, 10, 0, 11, 5, 7, 4),
    (11, 12, 10, 0, 3, 1, 9, 4, 7, 14, 5, 2, 6, 15, 13, 8),
    (13, 8, 5, 9, 4, 11, 7, 15, 0, 10, 3, 2, 14, 12, 6, 1),
    (7, 15, 11, 10, 14, 13, 5, 2, 6, 9, 12, 8, 1, 0, 4, 3),
    (14, 9, 8, 15, 12, 7, 6, 0, 4, 1, 11, 3, 10, 13, 5, 2),
    (4, 5, 9, 12, 15, 0, 3, 1, 7, 13, 14, 10, 11, 8, 6, 2),
    (3, 10, 0, 1, 14, 12, 8, 2, 4, 5, 7, 9, 6, 15, 11, 13),
    (8, 2, 3, 13, 6, 1, 10, 15, 11, 9, 5, 12, 14, 7, 4, 0),
    (0, 5, 4, 7, 2, 13, 11, 14, 3, 10, 8, 6, 1, 9, 15, 12),
)
PIECE_AT = np.argsort(np.array(PLACE), axis=1)
PIECE_WORDS = [
    [
        int(np.array(sum(int(p) << 4 * i for i, p in enumerate(row[at : at + 8])), np.uint32).astype(np.int32))
        for row in PIECE_AT
    ]
    for at in (0, 8)
]


def split(x):
    high = x.astype(jnp.bfloat16)
    low = (x - high.astype(jnp.float32)).astype(jnp.bfloat16)
    return high, low


def product(left, right):
    def one(x, y):
        return jnp.dot(x, y, preferred_element_type=jnp.float32)

    return one(left[0], right[0]) + (one(left[0], right[1]) + one(left[1], right[0]))


def chunk(index):
    return pl.ds(pl.multiple_of(index * NARROW, NARROW), NARROW)


def lines(a, b, j, start=0, count=NB):
    return pl.ds((a * NB + start) * STRIDE + j * 2 + b, count, stride=STRIDE)


def prepare_kernel(piece_ref, inverse_ref, kept_ref, high_ref, low_ref, inverse, sems):
    fetches = [
        pltpu.make_async_copy(inverse_ref, inverse, sems.at[0]),
        pltpu.make_async_copy(piece_ref, kept_ref, sems.at[1]),
    ]
    for fetch in fetches:
        fetch.start()
    fetches[0].wait()
    high_ref[...], low_ref[...] = split(inverse[...])
    fetches[1].wait()


def load_kernel(view_ref, tiles_ref, block, sems):
    fetches = [
        pltpu.make_async_copy(
            view_ref.at[pl.ds(a * NB * STRIDE, NB * STRIDE)],
            block.at[pl.ds(a * NB * STRIDE, NB * STRIDE)],
            sems.at[a],
        )
        for a in range(2)
    ]
    for fetch in fetches:
        fetch.start()
    for a in range(2):
        fetches[a].wait()
        for b in range(a + 1):
            for j in range(PARTS):
                tiles_ref[a + b, :, j * LANES : (j + 1) * LANES] = block[lines(a, b, j), :]


def meet_kernel(count, *refs):
    outs = refs[len(refs) - count :]
    for source, to in zip(refs[:count], outs):
        to[...] = source[...]


def stack_kernel(groups, *refs):
    sources = iter(refs)
    for group, out in zip(groups, refs[len(refs) - len(groups) :]):
        at = 0
        for count in group:
            out[at : at + count] = next(sources)[...]
            at += count


def left_kernel(
    steps, *refs,
):
    count = len(steps)
    blocks, others, (inv_high, inv_low) = refs[:count], refs[count : 2 * count], refs[2 * count : 2 * count + 2]
    high_ref, low_ref, own_ref, panel_high, panel_low, solved = refs[2 * count + 2 :]
    column = lax.axis_index("pcol")
    z, core = column // 2, column % 2
    for which in range(count):
        for slot, step in enumerate(steps[which]):
            chip = lax.rem(z + CHIPS_Z - step, CHIPS_Z)
            for source, where in ((blocks[which], core), (others[which], 1 - core)):
                rows = chunk(chip * 2 + where)
                for a in range(2):
                    panel_high[a, rows, :], panel_low[a, rows, :] = split(source[slot, a])
    for a in range(2):
        high, low = panel_high.at[a], panel_low.at[a]
        solved[:HALF, :] = product(
            (inv_high[:HALF, :HALF], inv_low[:HALF, :HALF]), (high[:HALF, :], low[:HALF, :])
        )
        solved[HALF:, :] = product(
            (inv_high[HALF:, :], inv_low[HALF:, :]), (high[...], low[...])
        )
        own_ref[0, a] = solved[chunk(column), :]
        high[...], low[...] = split(solved[...].T)
        high_ref[a, :, :HALF], low_ref[a, :, :HALF] = split(
            product((high[...], low[...]), (inv_high[:, :HALF], inv_low[:, :HALF]))
        )
        high_ref[a, :, HALF:], low_ref[a, :, HALF:] = split(
            product(
                (high[:, HALF:], low[:, HALF:]), (inv_high[HALF:, HALF:], inv_low[HALF:, HALF:])
            )
        )


def right_kernel(
    first_ref, second_ref, third_ref, fourth_ref, left_high, left_low, tiles_ref,
    updated_ref,
    block, panel_high, panel_low, out_sem,
):
    row = lax.axis_index("prow")
    column = lax.axis_index("pcol")
    beneath = row >= column
    y, x, core = row // SIDE, row % SIDE, column % 2

    def word(entries):
        picked = jnp.int32(0)
        for c, entry in enumerate(entries):
            picked = jnp.where(column == c, jnp.int32(entry), picked)
        return picked

    near, far = word(PIECE_WORDS[0]), word(PIECE_WORDS[1])

    def place(b):
        for group, source in enumerate((first_ref, second_ref, third_ref, fourth_ref)):
            for slot in range(SIDE):
                to_y = jnp.where(core == 0, OFFSETS[group], OFFSETS[slot])
                to_x = jnp.where(core == 0, OFFSETS[slot], OFFSETS[group])
                at = lax.rem(y + to_y + SIDE, SIDE) * SIDE + lax.rem(x + to_x + SIDE, SIDE)
                bits = lax.shift_right_logical(jnp.where(at < 8, near, far), at % 8 * 4)
                rows = chunk(bits & 15)
                panel_high[b, rows, :], panel_low[b, rows, :] = split(source[slot, b])

    def update(a, b, half):
        rows = slice(half * HALF, (half + 1) * HALF)
        change = product(
            (left_high[a, rows, :], left_low[a, rows, :]), (panel_high[b], panel_low[b])
        )
        result = tiles_ref[a + b, rows, :] - change
        for j in range(PARTS):
            block[lines(a, b, j, half * HALF, HALF), :] = result[:, j * LANES : (j + 1) * LANES]

    def clear(a, b, half):
        for j in range(PARTS):
            block[lines(a, b, j, half * HALF, HALF), :] = jnp.zeros((HALF, LANES), jnp.float32)

    def send(a, half):
        part = pl.ds((a * NB + half * HALF) * STRIDE, HALF * STRIDE)
        return pltpu.make_async_copy(
            block.at[part], updated_ref.at[part], out_sem.at[a * 2 + half]
        )

    place(0)
    for half in range(2):
        clear(0, 1, half)

        @pl.when(beneath)
        def _():
            update(0, 0, half)

        @pl.when(jnp.logical_not(beneath))
        def _():
            clear(0, 0, half)

        send(0, half).start()

    @pl.when(beneath)
    def _():
        place(1)

    for half in range(2):
        update(1, 0, half)

        @pl.when(beneath)
        def _():
            update(1, 1, half)

        @pl.when(jnp.logical_not(beneath))
        def _():
            clear(1, 1, half)

        send(1, half).start()
    for a in range(2):
        for half in range(2):
            send(a, half).wait()


VMEM = pl.BlockSpec(memory_space=pltpu.VMEM)
HBM = pl.BlockSpec(memory_space=pl.ANY)


def params(mib):
    return pltpu.CompilerParams(vmem_limit_bytes=mib * 1024 * 1024)


def along_z(step):
    return [(i, (i // 2 + step) % CHIPS_Z * 2 + i % 2) for i in range(GROUPS)]


def in_plane(move, piece):
    pairs = []
    for r in range(GROUPS):
        for c in range(GROUPS):
            dy, dx = move if c % 2 == 0 else move[::-1]
            to = (r // SIDE + dy) % SIDE * SIDE + (r % SIDE + dx) % SIDE
            pairs.append((r * GROUPS + c, to * GROUPS + c))
    return lax.ppermute(piece, ("prow", "pcol"), pairs)


def cost(flops, elements):
    return pl.CostEstimate(flops=flops, transcendentals=0, bytes_accessed=4 * elements)


def like(*arrays):
    return [jax.ShapeDtypeStruct(a.shape, a.dtype) for a in arrays]


def meet(pieces, others=(), hint=0):
    return pl.pallas_call(
        functools.partial(meet_kernel, len(pieces)),
        out_shape=like(*pieces),
        in_specs=[VMEM] * len(pieces) + [HBM] * len(others),
        out_specs=[VMEM] * len(pieces),
        compiler_params=params(4),
        cost_estimate=cost(0, hint or 2 * sum(p.size for p in pieces)),
        name="meet",
    )(*pieces, *others)


def stacked(*groups, others=(), hint=0):
    pieces = [p for group in groups for p in group]
    sizes = [[p.shape[0] for p in group] for group in groups]
    return pl.pallas_call(
        functools.partial(stack_kernel, sizes),
        out_shape=[
            jax.ShapeDtypeStruct((sum(size),) + group[0].shape[1:], jnp.float32)
            for size, group in zip(sizes, groups)
        ],
        in_specs=[VMEM] * len(pieces) + [HBM] * len(others),
        out_specs=[VMEM] * len(groups),
        compiler_params=params(4),
        cost_estimate=cost(0, hint or 2 * sum(p.size for p in pieces)),
        name="stack",
    )(*pieces, *others)


def local(trailing, panel, diag_inverse):
    piece = panel.transpose(0, 2, 1)[None]
    view = trailing.reshape(2, NB, 2, PARTS, LANES).transpose(0, 1, 3, 2, 4)
    view = view.reshape(2 * NB * STRIDE, LANES)
    whole = jax.ShapeDtypeStruct((NB, NB), jnp.bfloat16)
    pair = jax.ShapeDtypeStruct((2, NB, NB), jnp.bfloat16)

    def by(step, block):
        return lax.ppermute(block, "pcol", along_z(step))

    def swap(block):
        return lax.ppermute(block, "pcol", [(i, i ^ 1) for i in range(GROUPS)])

    kept, inv_high, inv_low = pl.pallas_call(
        prepare_kernel,
        out_shape=[*like(piece), whole, whole],
        in_specs=[pl.BlockSpec(memory_space=pltpu.HBM)] * 2,
        out_specs=[VMEM] * 3,
        scratch_shapes=[pltpu.VMEM((NB, NB), jnp.float32), pltpu.SemaphoreType.DMA((2,))],
        compiler_params=params(8),
        cost_estimate=cost(0, 2 * NB * NB),
        name="prepare",
    )(piece, diag_inverse)
    (tiles,) = pl.pallas_call(
        load_kernel,
        out_shape=[jax.ShapeDtypeStruct((3, NB, NB), jnp.float32)],
        in_specs=[HBM],
        out_specs=[VMEM],
        scratch_shapes=[pltpu.VMEM(view.shape, jnp.float32), pltpu.SemaphoreType.DMA((2,))],
        compiler_params=params(12),
        cost_estimate=cost(0, 8 * NB * NB),
        name="load",
    )(view)

    turn = [
        (r * GROUPS + c, PLACE[r][c] * GROUPS + r)
        for r in range(GROUPS)
        for c in range(GROUPS)
    ]
    turned = lax.ppermute(piece, ("prow", "pcol"), turn)
    one, seven = by(1, piece), by(-1, piece)
    two, six = by(1, one), by(-1, seven)
    (turned,) = meet([turned], hint=16777216)
    (turned,) = meet([turned], [inv_high, one, seven])
    planar = [in_plane(m, turned) for m in ((0, 1), (0, -1), (0, 2))]
    two, six = meet([two, six], [turned])
    three, five = by(1, two), by(-1, six)
    (first,) = stacked([turned] + planar, others=[two, six], hint=16777216)
    (same,) = stacked([kept, one, seven, two, six, three, five], others=[first])
    four = by(1, same[5:6])
    other, other_four = swap(same), swap(four)
    rest = [in_plane(m, first) for m in ((1, 0), (-1, 0), (2, 0))]
    left_high, left_low, own = pl.pallas_call(
        functools.partial(left_kernel, ((0, 1, 7, 2, 6, 3, 5), (4,))),
        out_shape=[pair, pair, *like(piece)],
        in_specs=[VMEM] * 6,
        out_specs=[VMEM] * 3,
        scratch_shapes=[
            pltpu.VMEM(pair.shape, pair.dtype),
            pltpu.VMEM(pair.shape, pair.dtype),
            pltpu.VMEM((NB, NB), jnp.float32),
        ],
        compiler_params=params(16),
        cost_estimate=cost(20 * NB**3, 6 * NB * NB),
        name="left",
    )(same, four, other, other_four, inv_high, inv_low)

    updated = pl.pallas_call(
        right_kernel,
        out_shape=jax.ShapeDtypeStruct(view.shape, jnp.float32),
        in_specs=[VMEM] * 7,
        out_specs=HBM,
        scratch_shapes=[
            pltpu.VMEM(view.shape, jnp.float32),
            pltpu.VMEM(pair.shape, pair.dtype),
            pltpu.VMEM(pair.shape, pair.dtype),
            pltpu.SemaphoreType.DMA((4,)),
        ],
        compiler_params=params(16),
        cost_estimate=cost(18 * NB**3, 12 * NB * NB),
        name="right",
    )(first, *rest, left_high, left_low, tiles)
    updated = updated.reshape(2, NB, PARTS, 2, LANES).transpose(0, 1, 3, 2, 4)
    return updated.reshape(trailing.shape), own[0].transpose(0, 2, 1)


def solution(mesh):
    return jax.shard_map(
        local,
        mesh=mesh,
        in_specs=(P(None, "prow", None, "pcol"), P(None, "prow", "pcol"), P()),
        out_specs=(P(None, "prow", None, "pcol"), P(None, "prow", "pcol")),
        check_vma=False,
    )
```

```python
import functools

import jax
import jax.numpy as jnp
import numpy as np
from jax import lax
from jax.experimental import pallas as pl
from jax.experimental.pallas import tpu as pltpu
from jax.sharding import PartitionSpec as P

CHIPS_Z = 8
SIDE = 4
GROUPS = 16
NB = 512
HALF = NB // 2
NARROW = 32
LANES = 128
PARTS = NB // LANES
STRIDE = 2 * PARTS
OFFSETS = (0, -1, 1, 2)
PLACE = (
    (7, 14, 6, 2, 11, 9, 5, 8, 12, 1, 0, 4, 13, 15, 3, 10),
    (1, 12, 4, 15, 10, 7, 14, 3, 2, 0, 13, 6, 5, 8, 9, 11),
    (15, 6, 11, 9, 8, 4, 12, 0, 7, 13, 1, 14, 10, 3, 2, 5),
    (9, 13, 1, 0, 5, 10, 11, 3, 6, 4, 2, 15, 12, 7, 14, 8),
    (1, 3, 13, 14, 8, 5, 10, 15, 2, 6, 9, 7, 4, 0, 11, 12),
    (0, 14, 12, 7, 15, 2, 13, 11, 5, 3, 10, 8, 1, 4, 9, 6),
    (5, 4, 15, 2, 6, 0, 1, 12, 8, 14, 11, 13, 3, 9, 7, 10),
    (2, 8, 3, 6, 1, 9, 13, 14, 12, 15, 10, 0, 11, 5, 7, 4),
    (11, 12, 10, 0, 3, 1, 9, 4, 7, 14, 5, 2, 6, 15, 13, 8),
    (13, 8, 5, 9, 4, 11, 7, 15, 0, 10, 3, 2, 14, 12, 6, 1),
    (7, 15, 11, 10, 14, 13, 5, 2, 6, 9, 12, 8, 1, 0, 4, 3),
    (14, 9, 8, 15, 12, 7, 6, 0, 4, 1, 11, 3, 10, 13, 5, 2),
    (4, 5, 9, 12, 15, 0, 3, 1, 7, 13, 14, 10, 11, 8, 6, 2),
    (3, 10, 0, 1, 14, 12, 8, 2, 4, 5, 7, 9, 6, 15, 11, 13),
    (8, 2, 3, 13, 6, 1, 10, 15, 11, 9, 5, 12, 14, 7, 4, 0),
    (0, 5, 4, 7, 2, 13, 11, 14, 3, 10, 8, 6, 1, 9, 15, 12),
)
PIECE_AT = np.argsort(np.array(PLACE), axis=1)
PIECE_WORDS = [
    [
        int(np.array(sum(int(p) << 4 * i for i, p in enumerate(row[at : at + 8])), np.uint32).astype(np.int32))
        for row in PIECE_AT
    ]
    for at in (0, 8)
]


def split(x):
    high = x.astype(jnp.bfloat16)
    low = (x - high.astype(jnp.float32)).astype(jnp.bfloat16)
    return high, low


def product(left, right):
    def one(x, y):
        return jnp.dot(x, y, preferred_element_type=jnp.float32)

    return one(left[0], right[0]) + (one(left[0], right[1]) + one(left[1], right[0]))


def chunk(index):
    return pl.ds(pl.multiple_of(index * NARROW, NARROW), NARROW)


def lines(a, b, j, start=0, count=NB):
    return pl.ds((a * NB + start) * STRIDE + j * 2 + b, count, stride=STRIDE)


def prepare_kernel(piece_ref, inverse_ref, kept_ref, high_ref, low_ref, inverse, sems):
    fetches = [
        pltpu.make_async_copy(inverse_ref, inverse, sems.at[0]),
        pltpu.make_async_copy(piece_ref, kept_ref, sems.at[1]),
    ]
    for fetch in fetches:
        fetch.start()
    fetches[0].wait()
    high_ref[...], low_ref[...] = split(inverse[...])
    fetches[1].wait()


def load_kernel(view_ref, tiles_ref, block, sems):
    fetches = [
        pltpu.make_async_copy(
            view_ref.at[pl.ds(a * NB * STRIDE, NB * STRIDE)],
            block.at[pl.ds(a * NB * STRIDE, NB * STRIDE)],
            sems.at[a],
        )
        for a in range(2)
    ]
    for fetch in fetches:
        fetch.start()
    for a in range(2):
        fetches[a].wait()
        for b in range(a + 1):
            for j in range(PARTS):
                tiles_ref[a + b, :, j * LANES : (j + 1) * LANES] = block[lines(a, b, j), :]


def meet_kernel(count, *refs):
    outs = refs[len(refs) - count :]
    for source, to in zip(refs[:count], outs):
        to[...] = source[...]


def stack_kernel(groups, *refs):
    sources = iter(refs)
    for group, out in zip(groups, refs[len(refs) - len(groups) :]):
        at = 0
        for count in group:
            out[at : at + count] = next(sources)[...]
            at += count


def left_kernel(
    steps, *refs,
):
    count = len(steps)
    blocks, others, (inv_high, inv_low) = refs[:count], refs[count : 2 * count], refs[2 * count : 2 * count + 2]
    high_ref, low_ref, own_ref, panel_high, panel_low, solved = refs[2 * count + 2 :]
    column = lax.axis_index("pcol")
    z, core = column // 2, column % 2
    for which in range(count):
        for slot, step in enumerate(steps[which]):
            chip = lax.rem(z + CHIPS_Z - step, CHIPS_Z)
            for source, where in ((blocks[which], core), (others[which], 1 - core)):
                rows = chunk(chip * 2 + where)
                for a in range(2):
                    panel_high[a, rows, :], panel_low[a, rows, :] = split(source[slot, a])
    for a in range(2):
        high, low = panel_high.at[a], panel_low.at[a]
        solved[:HALF, :] = product(
            (inv_high[:HALF, :HALF], inv_low[:HALF, :HALF]), (high[:HALF, :], low[:HALF, :])
        )
        solved[HALF:, :] = product(
            (inv_high[HALF:, :], inv_low[HALF:, :]), (high[...], low[...])
        )
        own_ref[0, a] = solved[chunk(column), :]
        high[...], low[...] = split(solved[...].T)
        high_ref[a, :, :HALF], low_ref[a, :, :HALF] = split(
            product((high[...], low[...]), (inv_high[:, :HALF], inv_low[:, :HALF]))
        )
        high_ref[a, :, HALF:], low_ref[a, :, HALF:] = split(
            product(
                (high[:, HALF:], low[:, HALF:]), (inv_high[HALF:, HALF:], inv_low[HALF:, HALF:])
            )
        )


def right_kernel(
    first_ref, second_ref, third_ref, fourth_ref, left_high, left_low, tiles_ref,
    updated_ref,
    block, panel_high, panel_low, out_sem,
):
    row = lax.axis_index("prow")
    column = lax.axis_index("pcol")
    beneath = row >= column
    y, x, core = row // SIDE, row % SIDE, column % 2

    def word(entries):
        picked = jnp.int32(0)
        for c, entry in enumerate(entries):
            picked = jnp.where(column == c, jnp.int32(entry), picked)
        return picked

    near, far = word(PIECE_WORDS[0]), word(PIECE_WORDS[1])

    def place(b):
        for group, source in enumerate((first_ref, second_ref, third_ref, fourth_ref)):
            for slot in range(SIDE):
                to_y = jnp.where(core == 0, OFFSETS[group], OFFSETS[slot])
                to_x = jnp.where(core == 0, OFFSETS[slot], OFFSETS[group])
                at = lax.rem(y + to_y + SIDE, SIDE) * SIDE + lax.rem(x + to_x + SIDE, SIDE)
                bits = lax.shift_right_logical(jnp.where(at < 8, near, far), at % 8 * 4)
                rows = chunk(bits & 15)
                panel_high[b, rows, :], panel_low[b, rows, :] = split(source[slot, b])

    def update(a, b, half):
        rows = slice(half * HALF, (half + 1) * HALF)
        change = product(
            (left_high[a, rows, :], left_low[a, rows, :]), (panel_high[b], panel_low[b])
        )
        result = tiles_ref[a + b, rows, :] - change
        for j in range(PARTS):
            block[lines(a, b, j, half * HALF, HALF), :] = result[:, j * LANES : (j + 1) * LANES]

    def clear(a, b, half):
        for j in range(PARTS):
            block[lines(a, b, j, half * HALF, HALF), :] = jnp.zeros((HALF, LANES), jnp.float32)

    def send(a, half):
        part = pl.ds((a * NB + half * HALF) * STRIDE, HALF * STRIDE)
        return pltpu.make_async_copy(
            block.at[part], updated_ref.at[part], out_sem.at[a * 2 + half]
        )

    place(0)
    for half in range(2):
        clear(0, 1, half)

        @pl.when(beneath)
        def _():
            update(0, 0, half)

        @pl.when(jnp.logical_not(beneath))
        def _():
            clear(0, 0, half)

        send(0, half).start()

    @pl.when(beneath)
    def _():
        place(1)

    for half in range(2):
        update(1, 0, half)

        @pl.when(beneath)
        def _():
            update(1, 1, half)

        @pl.when(jnp.logical_not(beneath))
        def _():
            clear(1, 1, half)

        send(1, half).start()
    for a in range(2):
        for half in range(2):
            send(a, half).wait()


VMEM = pl.BlockSpec(memory_space=pltpu.VMEM)
HBM = pl.BlockSpec(memory_space=pl.ANY)


def params(mib):
    return pltpu.CompilerParams(vmem_limit_bytes=mib * 1024 * 1024)


def along_z(step):
    return [(i, (i // 2 + step) % CHIPS_Z * 2 + i % 2) for i in range(GROUPS)]


def in_plane(move, piece):
    pairs = []
    for r in range(GROUPS):
        for c in range(GROUPS):
            dy, dx = move if c % 2 == 0 else move[::-1]
            to = (r // SIDE + dy) % SIDE * SIDE + (r % SIDE + dx) % SIDE
            pairs.append((r * GROUPS + c, to * GROUPS + c))
    return lax.ppermute(piece, ("prow", "pcol"), pairs)


def cost(flops, elements):
    return pl.CostEstimate(flops=flops, transcendentals=0, bytes_accessed=4 * elements)


def like(*arrays):
    return [jax.ShapeDtypeStruct(a.shape, a.dtype) for a in arrays]


def meet(pieces, others=(), hint=0):
    return pl.pallas_call(
        functools.partial(meet_kernel, len(pieces)),
        out_shape=like(*pieces),
        in_specs=[VMEM] * len(pieces) + [HBM] * len(others),
        out_specs=[VMEM] * len(pieces),
        compiler_params=params(4),
        cost_estimate=cost(0, hint or 2 * sum(p.size for p in pieces)),
        name="meet",
    )(*pieces, *others)


def stacked(*groups, others=(), hint=0):
    pieces = [p for group in groups for p in group]
    sizes = [[p.shape[0] for p in group] for group in groups]
    return pl.pallas_call(
        functools.partial(stack_kernel, sizes),
        out_shape=[
            jax.ShapeDtypeStruct((sum(size),) + group[0].shape[1:], jnp.float32)
            for size, group in zip(sizes, groups)
        ],
        in_specs=[VMEM] * len(pieces) + [HBM] * len(others),
        out_specs=[VMEM] * len(groups),
        compiler_params=params(4),
        cost_estimate=cost(0, hint or 2 * sum(p.size for p in pieces)),
        name="stack",
    )(*pieces, *others)


def local(trailing, panel, diag_inverse):
    piece = panel.transpose(0, 2, 1)[None]
    view = trailing.reshape(2, NB, 2, PARTS, LANES).transpose(0, 1, 3, 2, 4)
    view = view.reshape(2 * NB * STRIDE, LANES)
    whole = jax.ShapeDtypeStruct((NB, NB), jnp.bfloat16)
    pair = jax.ShapeDtypeStruct((2, NB, NB), jnp.bfloat16)

    def by(step, block):
        return lax.ppermute(block, "pcol", along_z(step))

    def swap(block):
        return lax.ppermute(block, "pcol", [(i, i ^ 1) for i in range(GROUPS)])

    kept, inv_high, inv_low = pl.pallas_call(
        prepare_kernel,
        out_shape=[*like(piece), whole, whole],
        in_specs=[pl.BlockSpec(memory_space=pltpu.HBM)] * 2,
        out_specs=[VMEM] * 3,
        scratch_shapes=[pltpu.VMEM((NB, NB), jnp.float32), pltpu.SemaphoreType.DMA((2,))],
        compiler_params=params(8),
        cost_estimate=cost(0, 2 * NB * NB),
        name="prepare",
    )(piece, diag_inverse)
    (tiles,) = pl.pallas_call(
        load_kernel,
        out_shape=[jax.ShapeDtypeStruct((3, NB, NB), jnp.float32)],
        in_specs=[HBM],
        out_specs=[VMEM],
        scratch_shapes=[pltpu.VMEM(view.shape, jnp.float32), pltpu.SemaphoreType.DMA((2,))],
        compiler_params=params(12),
        cost_estimate=cost(0, 8 * NB * NB),
        name="load",
    )(view)

    turn = [
        (r * GROUPS + c, PLACE[r][c] * GROUPS + r)
        for r in range(GROUPS)
        for c in range(GROUPS)
    ]
    turned = lax.ppermute(piece, ("prow", "pcol"), turn)
    one, seven = by(1, piece), by(-1, piece)
    two, six = by(1, one), by(-1, seven)
    (turned,) = meet([turned], hint=16777216)
    (turned,) = meet([turned], [inv_high, one, seven])
    planar = [in_plane(m, turned) for m in ((0, 1), (0, -1), (0, 2))]
    two, six = meet([two, six], [turned])
    three, five = by(1, two), by(-1, six)
    (first,) = stacked([turned] + planar, hint=16777216)
    (same,) = stacked([kept, one, seven, two, six, three, five], others=[first])
    four = by(1, same[5:6])
    other, other_four = swap(same), swap(four)
    rest = [in_plane(m, first) for m in ((1, 0), (-1, 0), (2, 0))]
    left_high, left_low, own = pl.pallas_call(
        functools.partial(left_kernel, ((0, 1, 7, 2, 6, 3, 5), (4,))),
        out_shape=[pair, pair, *like(piece)],
        in_specs=[VMEM] * 6,
        out_specs=[VMEM] * 3,
        scratch_shapes=[
            pltpu.VMEM(pair.shape, pair.dtype),
            pltpu.VMEM(pair.shape, pair.dtype),
            pltpu.VMEM((NB, NB), jnp.float32),
        ],
        compiler_params=params(16),
        cost_estimate=cost(20 * NB**3, 6 * NB * NB),
        name="left",
    )(same, four, other, other_four, inv_high, inv_low)

    updated = pl.pallas_call(
        right_kernel,
        out_shape=jax.ShapeDtypeStruct(view.shape, jnp.float32),
        in_specs=[VMEM] * 7,
        out_specs=HBM,
        scratch_shapes=[
            pltpu.VMEM(view.shape, jnp.float32),
            pltpu.VMEM(pair.shape, pair.dtype),
            pltpu.VMEM(pair.shape, pair.dtype),
            pltpu.SemaphoreType.DMA((4,)),
        ],
        compiler_params=params(16),
        cost_estimate=cost(18 * NB**3, 12 * NB * NB),
        name="right",
    )(first, *rest, left_high, left_low, tiles)
    updated = updated.reshape(2, NB, PARTS, 2, LANES).transpose(0, 1, 3, 2, 4)
    return updated.reshape(trailing.shape), own[0].transpose(0, 2, 1)


def solution(mesh):
    return jax.shard_map(
        local,
        mesh=mesh,
        in_specs=(P(None, "prow", None, "pcol"), P(None, "prow", "pcol"), P()),
        out_specs=(P(None, "prow", None, "pcol"), P(None, "prow", "pcol")),
        check_vma=False,
    )
```
